32 devices in a mesh: egrp: 4 (over y, x), inner: 8 (over z, core).
Axes of the slice: x: 2, y: 2, z: 4, core: 2. Of those that a mesh axis runs over, the one named last changes fastest.
Arguments:
- retarded: float32 [32, 2, 16, 128, 128], P(('egrp', 'inner')), may hold values from -0.31819806 to 0.31819806
- injection: float32 [32, 2, 16, 128, 128], P(('egrp', 'inner')), may hold values from -6 to 6
- coupling_matrices: float32 [2, 128, 128], replicated, may hold values from -0.5 to 0.5
- phonon_weight: float32 [2, 2], replicated, may hold values from 0.3 to 1
- phonon_shift: int32 [2], replicated, may hold values from 1 to 8, as said below
- slice_neighbour: int32 [16], replicated, may hold values from 0 to 15, as said below
Outputs:
- lesser_green: float32 [32, 2, 16, 128, 128], P(('egrp', 'inner'))
- phonon_sigma: float32 [32, 2, 16, 128, 128], P(('egrp', 'inner'))
The draws below stay inside these ranges and needn't reach their ends.
Inputs may be any that keep to these rules, and one draw needn't show every extreme that they name: `phonon_shift`: every entry is at least 1, and one entry equals 8. `slice_neighbour`: entry s is s - 1 or s + 1.
All inputs are finite; a program needn't handle non-finite values.
Results may differ from the reference program's by a relative error of at most 0.00015.
Values sent between devices are 32-bit elements; how exact they have to be, the bound alone decides.
A program may use at most 64 MiB of HBM per device.

```python
import math
import jax
import jax.numpy as jnp
from jax import lax

NO = 128
NS = 16
NMODE = 2
MAXSHIFT = 8
ITERS = 2
NE = 32


def draw_phonon_shift(key, part):
    first_key, second_key = jax.random.split(jax.random.fold_in(key, 11))
    chosen = jax.random.randint(first_key, (), 0, NMODE)
    others = jax.random.randint(second_key, (NMODE,), 1, MAXSHIFT + 1)
    return jnp.where(jnp.arange(NMODE) == chosen, MAXSHIFT, others).astype(jnp.int32)


def draw_slice_neighbour(key, part):
    leftward = jax.random.randint(jax.random.fold_in(key, 23), (NS,), 0, 2)
    slices = jnp.arange(NS)
    picked = jnp.where(leftward == 1, slices - 1, slices + 1)
    picked = jnp.where(slices == 0, 1, picked)
    picked = jnp.where(slices == NS - 1, NS - 2, picked)
    return picked.astype(jnp.int32)


def levels(stream_key, dims, cuts, least, high):
    loudness = 1.0
    for dim, shards_of in cuts:
        heights = jax.random.uniform(jax.random.fold_in(jax.random.fold_in(stream_key, 6), dim), (shards_of,), jnp.float32, least / len(cuts), high / len(cuts))
        loudness = loudness * jnp.repeat(jnp.exp(heights), dims[dim] // shards_of).reshape((-1,) + (1,) * (len(dims) - 1 - dim))
    return loudness


def scatter_about(key, shape, spread, bound, cuts=(), dtype=jnp.bfloat16):
    array = spread * jax.random.normal(key, shape, jnp.float32)
    if cuts:
        array = array * levels(key, shape, cuts, -0.22, 0.18)
    return jnp.clip(array, -bound, bound).astype(dtype)


def setup_inputs(seed: int = 0) -> dict:
    key_list = jax.random.split(jax.random.key(seed), 7)
    retarded = scatter_about(key_list[0], (NE, 2, NS, NO, NO), (0.6 * NO ** -0.5), 0.31819806, ((0, 32),), jnp.float32)
    injection = scatter_about(key_list[1], (NE, 2, NS, NO, NO), 1.0, 6.0, ((0, 32),), jnp.float32)
    coupling_matrices = scatter_about(key_list[2], (NMODE, NO, NO), NO ** -0.5, 0.5, (), jnp.float32)
    phonon_weight = jnp.clip(jnp.exp(jax.random.uniform(key_list[3], (NMODE, 2), jnp.float32, math.log(0.3), math.log(1.0))), 0.3, 1.0)
    phonon_shift = draw_phonon_shift(jax.random.fold_in(key_list[6], 71), 0)
    slice_neighbour = draw_slice_neighbour(jax.random.fold_in(key_list[6], 71), 0)
    return {"retarded": retarded, "injection": injection, "coupling_matrices": coupling_matrices, "phonon_weight": phonon_weight, "phonon_shift": phonon_shift, "slice_neighbour": slice_neighbour}


HIGHEST = lax.Precision.HIGHEST


def product(first, second):
    return jnp.einsum('eij,ejk->eik', first, second, precision=HIGHEST)


def product_adjoint(first, second):
    return jnp.einsum('eij,ekj->eik', first, second, precision=HIGHEST)


def sandwich(green_ret, source):
    real_green, imag_green = green_ret[:, 0], green_ret[:, 1]
    real_source, imag_source = source[:, 0], source[:, 1]
    real_inner = product(real_green, real_source) - product(imag_green, imag_source)
    imag_inner = product(real_green, imag_source) + product(imag_green, real_source)
    real_outer = product_adjoint(real_inner, real_green) + product_adjoint(imag_inner, imag_green)
    imag_outer = product_adjoint(imag_inner, real_green) - product_adjoint(real_inner, imag_green)
    return jnp.stack([real_outer, imag_outer], axis=1)


def couple(mixed_green, coupling_matrices, phonon_weight, phonon_shift):
    energies = mixed_green.shape[0]
    padded = jnp.pad(mixed_green, ((MAXSHIFT, MAXSHIFT), (0, 0), (0, 0), (0, 0)))
    accumulated = jnp.zeros_like(mixed_green)
    for phonon in range(NMODE):
        shifted_up = lax.dynamic_slice_in_dim(padded, (MAXSHIFT + phonon_shift[phonon]).astype(jnp.int32), energies, 0)
        shifted_down = lax.dynamic_slice_in_dim(padded, (MAXSHIFT - phonon_shift[phonon]).astype(jnp.int32), energies, 0)
        summed = phonon_weight[phonon, 0] * shifted_up + phonon_weight[phonon, 1] * shifted_down
        matrix = coupling_matrices[phonon]
        halfway = jnp.einsum('ij,ecjk->ecik', matrix, summed, precision=HIGHEST)
        accumulated = accumulated + jnp.einsum('ecik,lk->ecil', halfway, matrix, precision=HIGHEST)
    return accumulated


def reference(retarded, injection, coupling_matrices, phonon_weight, phonon_shift, slice_neighbour):
    green_slices = jnp.moveaxis(retarded, 2, 0)
    inject_slices = jnp.moveaxis(injection, 2, 0)
    phonon_sigma = jnp.zeros_like(green_slices)
    lesser = jnp.zeros_like(green_slices)
    for iteration in range(ITERS):
        lesser = lax.map(lambda operands: sandwich(operands[0], operands[1] + operands[2]),
                         (green_slices, inject_slices, phonon_sigma))
        mixed_green = lesser + 0.5 * jnp.take(lesser, slice_neighbour, axis=0)
        phonon_sigma = lax.map(lambda blocks: couple(blocks, coupling_matrices, phonon_weight, phonon_shift), mixed_green)
    return jnp.moveaxis(lesser, 0, 2), jnp.moveaxis(phonon_sigma, 0, 2)
```

```python
import functools

import jax
import jax.numpy as jnp
from jax import lax
from jax.experimental import pallas as pl
from jax.experimental.pallas import tpu as pltpu
from jax.sharding import PartitionSpec as P

MAXSHIFT = 8
ITERS = 2

MESH = pl.DeviceIdType.MESH
F32 = jnp.float32
BF16 = jnp.bfloat16


def halves(x):
    high = x.astype(BF16)
    return high, (x - high.astype(F32)).astype(BF16)


def dot3(first, second, dims):
    (first_high, first_low), (second_high, second_low) = first, second

    def one(a, b):
        return lax.dot_general(a, b, (dims, ((), ())), preferred_element_type=F32)

    return one(first_high, second_high) + (
        one(first_high, second_low) + one(first_low, second_high)
    )


PLAIN = ((1,), (0,))
ADJOINT = ((1,), (1,))


def kernel(
    groups, inner, pairs,
    ret_ref, inj_ref, coupling_ref, weight_ref, shift_ref, near_ref,
    lesser_ref, sigma_ref,
    mix_buf, k_buf, sig_buf,
    mix_send, mix_recv, sig_send, sig_recv, halo_send, halo_recv,
    *x_bufs,
):
    me = lax.axis_index("egrp") * inner + lax.axis_index("inner")
    group, mine = me // pairs, me % pairs
    my_slice, my_part = mine // 2, mine % 2
    slices = pairs // 2

    def device(flat):
        return (flat // inner, flat % inner)

    barrier = pltpu.get_barrier_semaphore()

    def greet(step, carry):
        other = group * pairs + (mine + step) % pairs
        pl.semaphore_signal(barrier, inc=1, device_id=device(other), device_id_type=MESH)
        return carry

    lax.fori_loop(1, pairs, greet, 0)
    if groups > 1:
        for side in (-1, 1):
            @pl.when((group + side >= 0) & (group + side < groups))
            def _():
                def greet_side(step, carry):
                    other = (group + side) * pairs + step
                    pl.semaphore_signal(
                        barrier, inc=1, device_id=device(other), device_id_type=MESH
                    )
                    return carry

                lax.fori_loop(0, pairs, greet_side, 0)

    zeros = jnp.zeros((MAXSHIFT,) + x_bufs[0].shape[1:], F32)
    for iteration in range(ITERS):
        @pl.when(group == 0)
        def _():
            x_bufs[iteration][pl.ds(0, MAXSHIFT)] = zeros

        @pl.when(group == groups - 1)
        def _():
            x_bufs[iteration][pl.ds(MAXSHIFT + pairs, MAXSHIFT)] = zeros

    def sandwich(iteration, s):
        source_real, source_imag = inj_ref[0, s], inj_ref[1, s]
        if iteration > 0:
            source_real = source_real + sig_buf[0, s]
            source_imag = source_imag + sig_buf[1, s]
        green_real, green_imag = halves(ret_ref[0, s]), halves(ret_ref[1, s])
        source_real, source_imag = halves(source_real), halves(source_imag)
        left = [jnp.concatenate([r, i], axis=1) for r, i in zip(green_real, green_imag)]
        middle = [
            jnp.concatenate(
                [jnp.concatenate([r, i], axis=1), jnp.concatenate([-i, r], axis=1)], axis=0
            )
            for r, i in zip(source_real, source_imag)
        ]
        right = [
            jnp.concatenate(
                [jnp.concatenate([r, i], axis=1), jnp.concatenate([-i, r], axis=1)], axis=0
            )
            for r, i in zip(green_real, green_imag)
        ]
        held = halves(dot3(left, middle, PLAIN))
        outer = dot3(held, right, ADJOINT)
        width = outer.shape[1] // 2
        lesser_ref[0, s] = outer[:, :width]
        lesser_ref[1, s] = outer[:, width:]

    def mix_copy(iteration, pair, owner):
        return pltpu.make_async_remote_copy(
            src_ref=mix_buf.at[iteration, pair],
            dst_ref=x_bufs[iteration].at[MAXSHIFT + owner],
            send_sem=mix_send.at[iteration, pair],
            recv_sem=mix_recv.at[iteration, owner],
            device_id=device(group * pairs + pair),
            device_id_type=MESH,
        )

    def halo_copy(iteration, side, pair):
        slot = mine % MAXSHIFT
        there = (MAXSHIFT + pairs if side == 0 else 0) + slot
        return pltpu.make_async_remote_copy(
            src_ref=mix_buf.at[iteration, pair],
            dst_ref=x_bufs[iteration].at[there],
            send_sem=halo_send.at[iteration, side, pair],
            recv_sem=halo_recv.at[iteration, side, slot],
            device_id=device((group + (1 if side else -1)) * pairs + pair),
            device_id_type=MESH,
        )

    def halo_arrival(iteration, side, slot):
        there = (MAXSHIFT + pairs if side == 0 else 0) + slot
        return pltpu.make_async_remote_copy(
            src_ref=mix_buf.at[iteration, 0],
            dst_ref=x_bufs[iteration].at[there],
            send_sem=halo_send.at[iteration, side, 0],
            recv_sem=halo_recv.at[iteration, side, slot],
            device_id=device(me),
            device_id_type=MESH,
        )

    def sends_halo(side):
        if side == 0:
            return (group > 0) & (mine < MAXSHIFT)
        return (group < groups - 1) & (mine >= pairs - MAXSHIFT)

    def gets_halo(side):
        return group < groups - 1 if side == 0 else group > 0

    def sigma_copy(iteration, energy, pair):
        target = sig_buf if iteration + 1 < ITERS else sigma_ref
        return pltpu.make_async_remote_copy(
            src_ref=k_buf.at[iteration, energy],
            dst_ref=target.at[pair % 2, pair // 2],
            send_sem=sig_send.at[iteration, energy],
            recv_sem=sig_recv.at[iteration, pair],
            device_id=device(group * pairs + energy),
            device_id_type=MESH,
        )

    coupling = [halves(coupling_ref[m]) for m in range(coupling_ref.shape[0])]
    wide = [jnp.concatenate(list(part), axis=1) for part in zip(*coupling)]

    def couple(iteration, energy):
        halfway = []
        for m in range(len(coupling)):
            shift = shift_ref[m]
            summed = (
                weight_ref[m, 0] * x_bufs[iteration][MAXSHIFT + energy + shift]
                + weight_ref[m, 1] * x_bufs[iteration][MAXSHIFT + energy - shift]
            )
            halfway.append(halves(dot3(coupling[m], halves(summed), PLAIN)))
        joined = [jnp.concatenate(list(part), axis=1) for part in zip(*halfway)]
        return dot3(joined, wide, ADJOINT)

    for iteration in range(ITERS):
        def do_sandwich(s, carry):
            sandwich(iteration, s)
            return carry

        lax.fori_loop(0, slices, do_sandwich, 0)

        if iteration == 0:
            if groups > 1:
                sides = (group > 0).astype(jnp.int32) + (group < groups - 1).astype(jnp.int32)
                pl.semaphore_wait(barrier, pairs - 1 + sides * pairs)
            else:
                pl.semaphore_wait(barrier, pairs - 1)

        def mixed(pair):
            part, s = pair % 2, pair // 2
            return lesser_ref[part, s] + 0.5 * lesser_ref[part, near_ref[s]]

        def do_mix(step, carry):
            pair = (mine + step) % pairs
            mix_buf[iteration, pair] = mixed(pair)
            mix_copy(iteration, pair, mine).start()
            if groups > 1:
                for side in (0, 1):
                    @pl.when(sends_halo(side))
                    def _():
                        halo_copy(iteration, side, pair).start()
            return carry

        lax.fori_loop(1, pairs, do_mix, 0)
        own = mixed(mine)
        x_bufs[iteration][MAXSHIFT + mine] = own
        if groups > 1:
            mix_buf[iteration, mine] = own
            for side in (0, 1):
                @pl.when(sends_halo(side))
                def _():
                    halo_copy(iteration, side, mine).start()

        def mix_arrives(step, carry):
            mix_copy(iteration, mine, (mine + pairs - step) % pairs).wait_recv()
            return carry

        lax.fori_loop(1, pairs, mix_arrives, 0)
        if groups > 1:
            for side in (0, 1):
                @pl.when(gets_halo(side))
                def _():
                    for slot in range(MAXSHIFT):
                        halo_arrival(iteration, side, slot).wait_recv()

        def do_couple(step, carry):
            energy = (mine + step) % pairs
            k_buf[iteration, energy] = couple(iteration, energy)
            sigma_copy(iteration, energy, mine).start()
            return carry

        lax.fori_loop(1, pairs, do_couple, 0)
        target = sig_buf if iteration + 1 < ITERS else sigma_ref
        target[my_part, my_slice] = couple(iteration, mine)

        def sigma_arrives(step, carry):
            sigma_copy(iteration, mine, (mine + pairs - step) % pairs).wait_recv()
            return carry

        lax.fori_loop(1, pairs, sigma_arrives, 0)

    def drain(step, carry):
        other = (mine + step) % pairs
        for iteration in range(ITERS):
            mix_copy(iteration, other, mine).wait_send()
            sigma_copy(iteration, other, mine).wait_send()
        return carry

    lax.fori_loop(1, pairs, drain, 0)
    if groups > 1:
        for side in (0, 1):
            @pl.when(sends_halo(side))
            def _():
                def drain_side(pair, carry):
                    for iteration in range(ITERS):
                        halo_copy(iteration, side, pair).wait_send()
                    return carry

                lax.fori_loop(0, pairs, drain_side, 0)


def local(groups, inner, retarded, injection, coupling_matrices, phonon_weight, phonon_shift, slice_neighbour):
    shape = retarded.shape[1:]
    block = shape[2:]
    pairs = shape[0] * shape[1]
    vmem = pl.BlockSpec(memory_space=pltpu.VMEM)
    smem = pl.BlockSpec(memory_space=pltpu.SMEM)
    sems = pltpu.SemaphoreType.DMA
    flops = ITERS * pairs * 8 * 3 * 2 * block[0] ** 3
    lesser, sigma = pl.pallas_call(
        functools.partial(kernel, groups, inner, pairs),
        out_shape=[jax.ShapeDtypeStruct(shape, F32)] * 2,
        in_specs=[vmem, vmem, vmem, smem, smem, smem],
        out_specs=[vmem, vmem],
        scratch_shapes=[
            pltpu.VMEM((ITERS, pairs) + block, F32),
            pltpu.VMEM((ITERS, pairs) + block, F32),
            pltpu.VMEM(shape, F32),
            sems((ITERS, pairs)),
            sems((ITERS, pairs)),
            sems((ITERS, pairs)),
            sems((ITERS, pairs)),
            sems((ITERS, 2, pairs if groups > 1 else 1)),
            sems((ITERS, 2, MAXSHIFT if groups > 1 else 1)),
            *[pltpu.VMEM((pairs + 2 * MAXSHIFT,) + block, F32) for _ in range(ITERS)],
        ],
        compiler_params=pltpu.CompilerParams(
            collective_id=0, has_side_effects=True, vmem_limit_bytes=48 * 1024 * 1024
        ),
        cost_estimate=pl.CostEstimate(
            flops=flops, bytes_accessed=4 * retarded.size * 4, transcendentals=0
        ),
    )(retarded[0], injection[0], coupling_matrices, phonon_weight, phonon_shift, slice_neighbour)
    return lesser[None], sigma[None]


def solution(mesh):
    inner = mesh.shape["inner"]
    devices = mesh.shape["egrp"] * inner
    spread = P(("egrp", "inner"), None, None, None, None)

    def run(retarded, *others):
        pairs = retarded.shape[1] * retarded.shape[2]
        groups = devices // pairs
        assert retarded.shape[0] == devices and devices == groups * pairs
        return jax.shard_map(
            functools.partial(local, groups, inner),
            mesh=mesh,
            in_specs=(spread, spread, P(), P(), P(), P()),
            out_specs=(spread, spread),
            check_vma=False,
        )(retarded, *others)

    return run
```

```python
import functools

import jax
import jax.numpy as jnp
from jax import lax
from jax.experimental import pallas as pl
from jax.experimental.pallas import tpu as pltpu
from jax.sharding import PartitionSpec as P

MAXSHIFT = 8
ITERS = 2

MESH = pl.DeviceIdType.MESH
F32 = jnp.float32
BF16 = jnp.bfloat16


def halves(x):
    high = x.astype(BF16)
    return high, (x - high.astype(F32)).astype(BF16)


def dot3(first, second, dims):
    (first_high, first_low), (second_high, second_low) = first, second

    def one(a, b):
        return lax.dot_general(a, b, (dims, ((), ())), preferred_element_type=F32)

    return one(first_high, second_high) + (
        one(first_high, second_low) + one(first_low, second_high)
    )


PLAIN = ((1,), (0,))
ADJOINT = ((1,), (1,))


def kernel(
    groups, inner, pairs,
    ret_ref, inj_ref, coupling_ref, weight_ref, shift_ref, near_ref,
    lesser_ref, sigma_ref,
    mix_buf, k_buf, sig_buf, z_buf,
    mix_send, mix_recv, sig_send, sig_recv, halo_send, halo_recv,
    *x_bufs,
):
    me = lax.axis_index("egrp") * inner + lax.axis_index("inner")
    group, mine = me // pairs, me % pairs
    my_slice, my_part = mine // 2, mine % 2
    slices = pairs // 2

    def device(flat):
        return (flat // inner, flat % inner)

    barrier = pltpu.get_barrier_semaphore()

    def greet(step, carry):
        other = group * pairs + (mine + step) % pairs
        pl.semaphore_signal(barrier, inc=1, device_id=device(other), device_id_type=MESH)
        return carry

    lax.fori_loop(1, pairs, greet, 0)
    if groups > 1:
        for side in (-1, 1):
            @pl.when((group + side >= 0) & (group + side < groups))
            def _():
                def greet_side(step, carry):
                    other = (group + side) * pairs + step
                    pl.semaphore_signal(
                        barrier, inc=1, device_id=device(other), device_id_type=MESH
                    )
                    return carry

                lax.fori_loop(0, pairs, greet_side, 0)

    zeros = jnp.zeros((MAXSHIFT,) + z_buf.shape[2:], F32)
    for m in range(z_buf.shape[0]):
        z_buf[m, pl.ds(0, MAXSHIFT)] = zeros
        z_buf[m, pl.ds(MAXSHIFT + pairs, MAXSHIFT)] = zeros

    def sandwich(iteration, s):
        source_real, source_imag = inj_ref[0, s], inj_ref[1, s]
        if iteration > 0:
            source_real = source_real + sig_buf[0, s]
            source_imag = source_imag + sig_buf[1, s]
        green_real, green_imag = halves(ret_ref[0, s]), halves(ret_ref[1, s])
        source_real, source_imag = halves(source_real), halves(source_imag)
        left = [jnp.concatenate([r, i], axis=1) for r, i in zip(green_real, green_imag)]
        middle = [
            jnp.concatenate(
                [jnp.concatenate([r, i], axis=1), jnp.concatenate([-i, r], axis=1)], axis=0
            )
            for r, i in zip(source_real, source_imag)
        ]
        right = [
            jnp.concatenate(
                [jnp.concatenate([r, i], axis=1), jnp.concatenate([-i, r], axis=1)], axis=0
            )
            for r, i in zip(green_real, green_imag)
        ]
        held = halves(dot3(left, middle, PLAIN))
        outer = dot3(held, right, ADJOINT)
        width = outer.shape[1] // 2
        lesser_ref[0, s] = outer[:, :width]
        lesser_ref[1, s] = outer[:, width:]

    def mix_copy(iteration, pair, owner):
        return pltpu.make_async_remote_copy(
            src_ref=mix_buf.at[iteration, pair],
            dst_ref=x_bufs[iteration].at[MAXSHIFT + owner],
            send_sem=mix_send.at[iteration, pair],
            recv_sem=mix_recv.at[iteration, owner],
            device_id=device(group * pairs + pair),
            device_id_type=MESH,
        )

    def halo_copy(iteration, side, pair):
        slot = mine % MAXSHIFT
        there = (MAXSHIFT + pairs if side == 0 else 0) + slot
        return pltpu.make_async_remote_copy(
            src_ref=mix_buf.at[iteration, pair],
            dst_ref=x_bufs[iteration].at[there],
            send_sem=halo_send.at[iteration, side, pair],
            recv_sem=halo_recv.at[iteration, side, slot],
            device_id=device((group + (1 if side else -1)) * pairs + pair),
            device_id_type=MESH,
        )

    def halo_arrival(iteration, side, slot):
        there = (MAXSHIFT + pairs if side == 0 else 0) + slot
        return pltpu.make_async_remote_copy(
            src_ref=mix_buf.at[iteration, 0],
            dst_ref=x_bufs[iteration].at[there],
            send_sem=halo_send.at[iteration, side, 0],
            recv_sem=halo_recv.at[iteration, side, slot],
            device_id=device(me),
            device_id_type=MESH,
        )

    def sends_halo(side):
        if side == 0:
            return (group > 0) & (mine < MAXSHIFT)
        return (group < groups - 1) & (mine >= pairs - MAXSHIFT)

    def gets_halo(side):
        return group < groups - 1 if side == 0 else group > 0

    def sigma_copy(iteration, energy, pair):
        target = sig_buf if iteration + 1 < ITERS else sigma_ref
        return pltpu.make_async_remote_copy(
            src_ref=k_buf.at[iteration, energy],
            dst_ref=target.at[pair % 2, pair // 2],
            send_sem=sig_send.at[iteration, energy],
            recv_sem=sig_recv.at[iteration, pair],
            device_id=device(group * pairs + energy),
            device_id_type=MESH,
        )

    modes = coupling_ref.shape[0]
    size = coupling_ref.shape[1]
    coupling = [halves(coupling_ref[m]) for m in range(modes)]
    tall = [jnp.concatenate(list(part), axis=0) for part in zip(*coupling)]

    def project(iteration, slots):
        blocks = [halves(x_bufs[iteration][slot]) for slot in slots]
        side = [jnp.concatenate(list(part), axis=1) for part in zip(*blocks)]
        halfway = halves(dot3(tall, side, PLAIN))
        for m in range(modes):
            rows = slice(m * size, (m + 1) * size)
            stacked = [
                jnp.concatenate(
                    [part[rows, i * size:(i + 1) * size] for i in range(len(slots))], axis=0
                )
                for part in halfway
            ]
            done = dot3(stacked, coupling[m], ADJOINT)
            for i, slot in enumerate(slots):
                z_buf[m, slot] = done[i * size:(i + 1) * size]

    def couple(energy):
        total = None
        for m in range(modes):
            shift = shift_ref[m]
            term = (
                weight_ref[m, 0] * z_buf[m, MAXSHIFT + energy + shift]
                + weight_ref[m, 1] * z_buf[m, MAXSHIFT + energy - shift]
            )
            total = term if total is None else total + term
        return total

    for iteration in range(ITERS):
        way = 1 if iteration % 2 == 0 else -1

        def slice_at(step):
            return (my_slice + way * step + slices) % slices

        def mixed(pair):
            part, s = pair % 2, pair // 2
            return lesser_ref[part, s] + 0.5 * lesser_ref[part, near_ref[s]]

        def send_mixed(pair):
            mix_buf[iteration, pair] = mixed(pair)
            mix_copy(iteration, pair, mine).start()
            if groups > 1:
                for side in (0, 1):
                    @pl.when(sends_halo(side))
                    def _():
                        halo_copy(iteration, side, pair).start()

        def do_sandwich(step, carry):
            s = slice_at(step)
            if iteration > 0:
                for part in range(2):
                    sigma_copy(iteration - 1, mine, 2 * s + part).wait_recv()
            sandwich(iteration, s)
            return carry

        def do_slice(step, carry):
            do_sandwich(step, carry)
            s = slice_at(step - 1)
            for part in range(2):
                send_mixed(2 * s + part)
            return carry

        if iteration > 0:
            sigma_copy(iteration - 1, mine, 2 * my_slice + 1 - my_part).wait_recv()
        sandwich(iteration, my_slice)
        do_sandwich(1, 0)
        if iteration == 0:
            if groups > 1:
                sides = (group > 0).astype(jnp.int32) + (group < groups - 1).astype(jnp.int32)
                pl.semaphore_wait(barrier, pairs - 1 + sides * pairs)
            else:
                pl.semaphore_wait(barrier, pairs - 1)
        lax.fori_loop(2, slices, do_slice, 0)
        for part in range(2):
            send_mixed(2 * slice_at(slices - 1) + part)
        send_mixed(2 * my_slice + 1 - my_part)
        own = mixed(mine)
        x_bufs[iteration][MAXSHIFT + mine] = own
        if groups > 1:
            mix_buf[iteration, mine] = own
            for side in (0, 1):
                @pl.when(sends_halo(side))
                def _():
                    halo_copy(iteration, side, mine).start()

        def source_at(step):
            return (mine - way * step + pairs) % pairs

        def arrival(step):
            mix_copy(iteration, mine, source_at(step)).wait_recv()

        def project_at(step):
            project(iteration, [MAXSHIFT + source_at(step), MAXSHIFT + source_at(step + 1)])

        def do_project(step, carry):
            arrival(2 * step)
            arrival(2 * step + 1)
            project_at(2 * step)
            return carry

        arrival(1)
        project_at(0)
        lax.fori_loop(1, slices, do_project, 0)
        if groups > 1:
            for side in (0, 1):
                @pl.when(gets_halo(side))
                def _():
                    start = MAXSHIFT + pairs if side == 0 else 0
                    for slot in range(MAXSHIFT):
                        halo_arrival(iteration, side, slot).wait_recv()
                        project(iteration, [start + slot])

        def do_couple(step, carry):
            energy = (mine + step) % pairs
            k_buf[iteration, energy] = couple(energy)
            sigma_copy(iteration, energy, mine).start()
            return carry

        lax.fori_loop(1, pairs, do_couple, 0)
        target = sig_buf if iteration + 1 < ITERS else sigma_ref
        target[my_part, my_slice] = couple(mine)

    def sigma_arrives(step, carry):
        sigma_copy(ITERS - 1, mine, (mine + pairs - step) % pairs).wait_recv()
        return carry

    lax.fori_loop(1, pairs, sigma_arrives, 0)

    def drain(step, carry):
        other = (mine + step) % pairs
        for iteration in range(ITERS):
            mix_copy(iteration, other, mine).wait_send()
            sigma_copy(iteration, other, mine).wait_send()
        return carry

    lax.fori_loop(1, pairs, drain, 0)
    if groups > 1:
        for side in (0, 1):
            @pl.when(sends_halo(side))
            def _():
                def drain_side(pair, carry):
                    for iteration in range(ITERS):
                        halo_copy(iteration, side, pair).wait_send()
                    return carry

                lax.fori_loop(0, pairs, drain_side, 0)


def local(groups, inner, retarded, injection, coupling_matrices, phonon_weight, phonon_shift, slice_neighbour):
    shape = retarded.shape[1:]
    block = shape[2:]
    pairs = shape[0] * shape[1]
    modes = coupling_matrices.shape[0]
    vmem = pl.BlockSpec(memory_space=pltpu.VMEM)
    smem = pl.BlockSpec(memory_space=pltpu.SMEM)
    sems = pltpu.SemaphoreType.DMA
    flops = ITERS * pairs * 8 * 3 * 2 * block[0] ** 3
    lesser, sigma = pl.pallas_call(
        functools.partial(kernel, groups, inner, pairs),
        out_shape=[jax.ShapeDtypeStruct(shape, F32)] * 2,
        in_specs=[vmem, vmem, vmem, smem, smem, smem],
        out_specs=[vmem, vmem],
        scratch_shapes=[
            pltpu.VMEM((ITERS, pairs) + block, F32),
            pltpu.VMEM((ITERS, pairs) + block, F32),
            pltpu.VMEM(shape, F32),
            pltpu.VMEM((modes, pairs + 2 * MAXSHIFT) + block, F32),
            sems((ITERS, pairs)),
            sems((ITERS, pairs)),
            sems((ITERS, pairs)),
            sems((ITERS, pairs)),
            sems((ITERS, 2, pairs if groups > 1 else 1)),
            sems((ITERS, 2, MAXSHIFT if groups > 1 else 1)),
            *[pltpu.VMEM((pairs + 2 * MAXSHIFT,) + block, F32) for _ in range(ITERS)],
        ],
        compiler_params=pltpu.CompilerParams(
            collective_id=0, has_side_effects=True, vmem_limit_bytes=48 * 1024 * 1024
        ),
        cost_estimate=pl.CostEstimate(
            flops=flops, bytes_accessed=4 * retarded.size * 4, transcendentals=0
        ),
    )(retarded[0], injection[0], coupling_matrices, phonon_weight, phonon_shift, slice_neighbour)
    return lesser[None], sigma[None]


def solution(mesh):
    inner = mesh.shape["inner"]
    devices = mesh.shape["egrp"] * inner
    spread = P(("egrp", "inner"), None, None, None, None)

    def run(retarded, *others):
        pairs = retarded.shape[1] * retarded.shape[2]
        groups = devices // pairs
        assert retarded.shape[0] == devices and devices == groups * pairs
        return jax.shard_map(
            functools.partial(local, groups, inner),
            mesh=mesh,
            in_specs=(spread, spread, P(), P(), P(), P()),
            out_specs=(spread, spread),
            check_vma=False,
        )(retarded, *others)

    return run
```
